32 devices in a mesh: ctx: 16 (over z, x, core), head: 2 (over y).
Axes of the slice: x: 2, y: 2, z: 4, core: 2. Of those that a mesh axis runs over, the one named last changes fastest.
Arguments:
- q_latent: bfloat16 [2048, 64, 512], P('ctx', 'head'), may hold values from -1.25 to 1.25
- q_rope: bfloat16 [2048, 4096], P('ctx', 'head'), may hold values from -1.25 to 1.25
- attn_out: bfloat16 [2048, 64, 512], P('ctx', 'head'), may hold values from -4 to 4
- grad_out: bfloat16 [2048, 64, 512], P('ctx', 'head'), may hold values from -1 to 1
- log_total: float32 [2048, 64], P('ctx', 'head'), may hold values from 4 to 6
- latent: bfloat16 [2048, 512], P('ctx'), may hold values from -2.5 to 2.5
- key_rope: bfloat16 [2048, 64], P('ctx'), may hold values from -2.5 to 2.5
- doc_start: int32 [2048], P('ctx'), may hold values from 0 to 2047, as said below
Outputs:
- grad_q_latent: bfloat16 [2048, 64, 512], P('ctx', 'head')
- grad_q_rope: bfloat16 [2048, 4096], P('ctx', 'head')
- grad_latent: bfloat16 [2048, 512], P(('ctx', 'head'))
- grad_key_rope: bfloat16 [2048, 64], P(('ctx', 'head'))
The draws below stay inside these ranges and needn't reach their ends.
Inputs may be any that keep to these rules, and one draw needn't show every extreme that they name: doc_start[t] is the first token of the document that holds token t. Documents are runs of 1 to 897 tokens laid end to end from token 0; one document has exactly 897 tokens, and the last token of the sequence is a document of its own.
All inputs are finite; a program needn't handle non-finite values.
Results may differ from the reference program's by a relative error of at most 0.0056.
Values may be sent and summed in bfloat16 or wider, within the bound.
A program may use at most 128 MiB of HBM per device.

```python
import jax
import jax.numpy as jnp
from jax import lax

LAT = 512
ROPE = 64
NOPE = 128
HEADS = 64
TOK_DEV = 128
LEVELS = 3
DOC_MAX = 897
TOKENS = 2048
N_CTX = 16


def draw_doc_start(key, part):
    base_key = jax.random.fold_in(key, 11)
    key_len, key_long = jax.random.split(base_key)
    lengths = jax.random.randint(key_len, (TOKENS,), 1, DOC_MAX + 1, dtype=jnp.int32)
    long_index = jax.random.randint(key_long, (), 0, TOKENS // DOC_MAX - 1, dtype=jnp.int32)
    lengths = jnp.where(jnp.arange(TOKENS, dtype=jnp.int32) == long_index, DOC_MAX, lengths)
    doc_ends = jnp.cumsum(lengths).astype(jnp.int32)
    positions = jnp.arange(TOKENS, dtype=jnp.int32)
    doc_index = jnp.searchsorted(doc_ends, positions, side='right')
    doc_starts = (doc_ends - lengths)[doc_index]
    doc_starts = jnp.where(positions == TOKENS - 1, TOKENS - 1, doc_starts)
    return doc_starts.astype(jnp.int32)


def steps_of(rng, shape, shards, low, top_value):
    loudness = 1.0
    for dim, blocks in shards:
        draws = jax.random.uniform(jax.random.fold_in(jax.random.fold_in(rng, 6), dim), (blocks,), jnp.float32, low / len(shards), top_value / len(shards))
        loudness = loudness * jnp.repeat(jnp.exp(draws), shape[dim] // blocks).reshape((-1,) + (1,) * (len(shape) - 1 - dim))
    return loudness


def scatter_about(own_key, extent, deviation, reach, cuts=(), kind=jnp.bfloat16):
    gain = steps_of(own_key, extent, cuts, -0.22, 0.18) if cuts else 1.0
    result = jax.random.normal(own_key, extent, jnp.float32) * deviation * gain
    return jnp.minimum(jnp.maximum(result, -reach), reach).astype(kind)


def setup_inputs(seed: int = 0) -> dict:
    seeds = jax.random.split(jax.random.key(seed), 9)
    return {
        "q_latent": scatter_about(seeds[0], (TOKENS, HEADS, LAT), 0.5, 1.25, ((0, 16), (1, 2))),
        "q_rope": scatter_about(seeds[1], (TOKENS, HEADS * ROPE), 0.5, 1.25, ((0, 16), (1, 2))),
        "attn_out": scatter_about(seeds[2], (TOKENS, HEADS, LAT), 1.0, 4.0, ((0, 16), (1, 2))),
        "grad_out": scatter_about(seeds[3], (TOKENS, HEADS, LAT), 0.2, 1.0, ((0, 16), (1, 2))),
        "log_total": jnp.clip(4.0 + 2.0 * jax.random.uniform(seeds[4], (TOKENS, HEADS), jnp.float32) ** steps_of(seeds[4], (TOKENS, HEADS), ((0, 16), (1, 2)), -0.2, 0.2), 4.0, 6.0),
        "latent": scatter_about(seeds[5], (TOKENS, LAT), 1.0, 2.5, ((0, 16),)),
        "key_rope": scatter_about(seeds[6], (TOKENS, ROPE), 1.0, 2.5, ((0, 16),)),
        "doc_start": draw_doc_start(jax.random.fold_in(seeds[8], 71), 0),
    }


def tile_terms(q_lat, q_rot, grad_rows, row_delta, log_rows, starts, query_pos, latent_blk, rope_blk, key_first, softmax_scale):
    key_pos = key_first + jnp.arange(latent_blk.shape[0], dtype=jnp.int32)
    visible = ((key_pos[None, :] >= starts[:, None]) & (key_pos[None, :] <= query_pos[:, None]))[:, None, :]
    q_wide = q_lat.astype(jnp.float32)
    rot_wide = q_rot.astype(jnp.float32)
    grad_wide = grad_rows.astype(jnp.float32)
    lat_wide = latent_blk.astype(jnp.float32)
    key_wide = rope_blk.astype(jnp.float32)
    scores = (jnp.einsum('thc,kc->thk', q_wide, lat_wide) + jnp.einsum('thr,kr->thk', rot_wide, key_wide)) * softmax_scale
    probs = jnp.where(visible, jnp.exp(jnp.where(visible, scores, 0.0) - log_rows[:, :, None]), 0.0)
    grad_probs = jnp.einsum('thc,kc->thk', grad_wide, lat_wide)
    grad_scores = probs * (grad_probs - row_delta[:, :, None])
    probs_b = lax.optimization_barrier(probs.astype(jnp.bfloat16)).astype(jnp.float32)
    grad_b = lax.optimization_barrier(grad_scores.astype(jnp.bfloat16)).astype(jnp.float32)
    grad_qlat = softmax_scale * jnp.einsum('thk,kc->thc', grad_b, lat_wide)
    grad_qrot = softmax_scale * jnp.einsum('thk,kr->thr', grad_b, key_wide)
    grad_lat = softmax_scale * jnp.einsum('thk,thc->kc', grad_b, q_wide) + jnp.einsum('thk,thc->kc', probs_b, grad_wide)
    grad_rot = softmax_scale * jnp.einsum('thk,thr->kr', grad_b, rot_wide)
    return grad_qlat, grad_qrot, grad_lat, grad_rot


def reference(q_latent, q_rope, attn_out, grad_out, log_total, latent, key_rope, doc_start):
    tiles = N_CTX
    span = 2 ** LEVELS
    softmax_scale = (NOPE + ROPE) ** -0.5
    q_lat = q_latent.reshape(tiles, TOK_DEV, HEADS, LAT)
    q_rot = q_rope.reshape(tiles, TOK_DEV, HEADS, ROPE)
    grad_rows = grad_out.reshape(tiles, TOK_DEV, HEADS, LAT)
    out_rows = attn_out.reshape(tiles, TOK_DEV, HEADS, LAT)
    log_rows = log_total.reshape(tiles, TOK_DEV, HEADS)
    starts = doc_start.reshape(tiles, TOK_DEV)
    pad_lat = jnp.concatenate([jnp.zeros((span - 1, TOK_DEV, LAT), latent.dtype), latent.reshape(tiles, TOK_DEV, LAT)], 0)
    pad_rot = jnp.concatenate([jnp.zeros((span - 1, TOK_DEV, ROPE), key_rope.dtype), key_rope.reshape(tiles, TOK_DEV, ROPE)], 0)

    def per_tile(tile_index):
        own_q = q_lat[tile_index]
        own_rot = q_rot[tile_index]
        own_grad = grad_rows[tile_index]
        own_log = log_rows[tile_index]
        own_starts = starts[tile_index]
        row_delta = jnp.einsum('thc,thc->th', own_grad.astype(jnp.float32), out_rows[tile_index].astype(jnp.float32))
        query_pos = tile_index * TOK_DEV + jnp.arange(TOK_DEV, dtype=jnp.int32)
        earliest = jnp.min(own_starts)

        def visit(totals, offset):
            key_tile = tile_index - (span - 1) + offset
            latent_blk = lax.dynamic_index_in_dim(pad_lat, tile_index + offset, 0, keepdims=False)
            rope_blk = lax.dynamic_index_in_dim(pad_rot, tile_index + offset, 0, keepdims=False)
            key_first = key_tile * TOK_DEV

            def compute(unused):
                return tile_terms(own_q, own_rot, own_grad, row_delta, own_log, own_starts, query_pos, latent_blk, rope_blk, key_first, softmax_scale)

            def skipped(unused):
                return (jnp.zeros((TOK_DEV, HEADS, LAT), jnp.float32), jnp.zeros((TOK_DEV, HEADS, ROPE), jnp.float32),
                        jnp.zeros((TOK_DEV, LAT), jnp.float32), jnp.zeros((TOK_DEV, ROPE), jnp.float32))

            terms = lax.cond(earliest <= key_first + TOK_DEV - 1, compute, skipped, 0)
            return (totals[0] + terms[0], totals[1] + terms[1]), (terms[2], terms[3])

        init = (jnp.zeros((TOK_DEV, HEADS, LAT), jnp.float32), jnp.zeros((TOK_DEV, HEADS, ROPE), jnp.float32))
        totals, parts = lax.scan(visit, init, jnp.arange(span, dtype=jnp.int32))
        return (totals[0].astype(jnp.bfloat16), totals[1].astype(jnp.bfloat16)), parts

    (grad_qlat, grad_qrot), (part_lat, part_rot) = lax.map(per_tile, jnp.arange(tiles, dtype=jnp.int32))
    grad_lat = jnp.zeros((tiles + span - 1, TOK_DEV, LAT), jnp.float32)
    grad_rot = jnp.zeros((tiles + span - 1, TOK_DEV, ROPE), jnp.float32)
    for offset in range(span):
        grad_lat = grad_lat.at[offset:offset + tiles].add(part_lat[:, offset])
        grad_rot = grad_rot.at[offset:offset + tiles].add(part_rot[:, offset])
    grad_lat = grad_lat[span - 1:]
    grad_rot = grad_rot[span - 1:]
    return (grad_qlat.reshape(TOKENS, HEADS, LAT),
            grad_qrot.reshape(TOKENS, HEADS * ROPE),
            grad_lat.reshape(TOKENS, LAT).astype(jnp.bfloat16),
            grad_rot.reshape(TOKENS, ROPE).astype(jnp.bfloat16))
```

```python
import functools

import jax
import jax.numpy as jnp
from jax import lax
from jax.experimental import pallas as pl
from jax.experimental.pallas import tpu as pltpu
from jax.sharding import PartitionSpec as P

ROPE = 64
NOPE = 128
LEVELS = 3
SPAN = 2**LEVELS
SCALE = (NOPE + ROPE) ** (-0.5)
LOG2E = 1.4426950408889634
ORDER = (0, 3, 4, 5, 6, 7, 1, 2)
GROUP = 2
BLOCK = 512
HIDDEN = -1e30
MESH = pl.DeviceIdType.MESH


def dot_nt(a, b):
    return lax.dot_general(a, b, (((1,), (1,)), ((), ())), preferred_element_type=jnp.float32)


def dot_tn(a, b):
    return lax.dot_general(a, b, (((0,), (0,)), ((), ())), preferred_element_type=jnp.float32)


def dot_nn(a, b):
    return lax.dot_general(a, b, (((1,), (0,)), ((), ())), preferred_element_type=jnp.float32)


def kernel(
    n_ctx,
    n_head,
    tok,
    heads,
    lat,
    q_hbm,
    qr_hbm,
    ao_hbm,
    go_hbm,
    lt_hbm,
    kv_own,
    starts,
    gq_hbm,
    gqr_hbm,
    gkv_out,
    q,
    qr,
    go,
    ao,
    lt,
    delta,
    kv,
    bias,
    acc,
    gacc,
    part,
    recv,
    total,
    gq,
    gqr,
    in_sem,
    out_sem,
    kv_send,
    kv_recv,
    p_send,
    p_recv,
):
    me = lax.axis_index("ctx")
    my_head = lax.axis_index("head")
    rows = tok * heads
    block = min(BLOCK, rows)
    count = rows // block
    tok_blk = block // heads
    piece = tok // n_head
    width = GROUP * tok
    slot_of = {dist: place for place, dist in enumerate(ORDER)}

    barrier = pltpu.get_barrier_semaphore()
    for dist in range(-(SPAN - 1), SPAN):
        for turn in range(n_head):
            if dist == 0 and turn == 0:
                continue

            @pl.when((me + dist >= 0) & (me + dist < n_ctx))
            def _():
                pl.semaphore_signal(
                    barrier,
                    inc=1,
                    device_id=(me + dist, lax.rem(my_head + turn, n_head)),
                    device_id_type=MESH,
                )

    def load(b):
        rng = pl.ds(b * block, block)
        return [
            pltpu.make_async_copy(src.at[rng], dst.at[rng], in_sem.at[i, b])
            for i, (src, dst) in enumerate(
                ((go_hbm, go), (ao_hbm, ao), (q_hbm, q), (qr_hbm, qr), (lt_hbm, lt))
            )
        ]

    for b in range(count):
        for copy in load(b):
            copy.start()

    reach = jnp.minimum(me, SPAN - 1) + jnp.minimum(n_ctx - 1 - me, SPAN - 1) + 1
    pl.semaphore_wait(barrier, reach * n_head - 1)

    def kv_copy(dist):
        return pltpu.make_async_remote_copy(
            src_ref=kv_own,
            dst_ref=kv.at[pl.ds(slot_of[dist] * tok, tok)],
            send_sem=kv_send.at[dist],
            recv_sem=kv_recv.at[dist],
            device_id=(me + dist, my_head),
            device_id_type=MESH,
        )

    for dist in ORDER[1:]:

        @pl.when(me + dist < n_ctx)
        def _():
            kv_copy(dist).start()

    kv[pl.ds(0, tok)] = kv_own[...]
    for dist in ORDER[1:]:

        @pl.when(me < dist)
        def _():
            kv[pl.ds(slot_of[dist] * tok, tok)] = jnp.zeros((tok, kv.shape[1]), kv.dtype)

    query_pos = me * tok + lax.broadcasted_iota(jnp.int32, (tok, tok), 0)
    lane = lax.broadcasted_iota(jnp.int32, (tok, tok), 1)
    for place, dist in enumerate(ORDER):
        key_pos = (me - dist) * tok + lane
        seen = (key_pos >= starts[...]) & (key_pos <= query_pos)
        bias[place // GROUP, :, pl.ds((place % GROUP) * tok, tok)] = jnp.where(seen, 0.0, HIDDEN)

    def part_copy(dist, turn):
        target = lax.rem(my_head + turn, n_head)
        return pltpu.make_async_remote_copy(
            src_ref=part.at[pl.ds(pl.multiple_of(slot_of[dist] * tok + target * piece, piece), piece)],
            dst_ref=recv.at[dist * n_head + turn],
            send_sem=p_send.at[dist * n_head + turn],
            recv_sem=p_recv.at[dist * n_head + turn],
            device_id=(me - dist, target),
            device_id_type=MESH,
        )

    groups = SPAN // GROUP
    for g in range(groups):
        for dist in ORDER[g * GROUP : (g + 1) * GROUP]:
            if dist:

                @pl.when(me >= dist)
                def _():
                    kv_copy(dist).wait_recv()

        gacc[...] = jnp.zeros_like(gacc)

        def step(b, unused):
            start = pl.multiple_of(b * block, block)
            rng = pl.ds(start, block)
            if g == 0:
                for copy in load(b):
                    copy.wait()
                d = jnp.sum(
                    go[rng, :].astype(jnp.float32) * ao[rng, :].astype(jnp.float32),
                    axis=1,
                    keepdims=True,
                )
                delta[rng, :] = jnp.broadcast_to(d * SCALE, (block, 128))
            keys = kv[pl.ds(g * width, width), :]
            q_b, qr_b, go_b = q[rng, :], qr[rng, :], go[rng, :]
            scores = dot_nt(q_b, keys[:, :lat]) + dot_nt(qr_b, keys[:, lat:])
            grad_probs = dot_nt(go_b, keys[:, :lat])
            hide = bias[g, pl.ds(pl.multiple_of(b * tok_blk, tok_blk), tok_blk), :]
            hide = jnp.broadcast_to(hide[:, None, :], (tok_blk, heads, width)).reshape(block, width)
            times = width // 128
            lt_b = jnp.concatenate([lt[rng, :]] * times, axis=1)
            d_b = jnp.concatenate([delta[rng, :]] * times, axis=1)
            probs = jnp.exp2(scores * (SCALE * LOG2E) - lt_b + hide)
            grads = probs * (grad_probs * SCALE - d_b)
            probs_b = probs.astype(jnp.bfloat16)
            grad_b = grads.astype(jnp.bfloat16)
            gq_b = dot_nn(grad_b, keys)
            if g > 0:
                gq_b = acc[rng, :] + gq_b
            if g < groups - 1:
                acc[rng, :] = gq_b
            else:
                gq[rng, :] = gq_b[:, :lat].astype(jnp.bfloat16)
                gqr[rng, :] = gq_b[:, lat:].astype(jnp.bfloat16)
                pltpu.make_async_copy(gq.at[rng], gq_hbm.at[rng], out_sem.at[0, b]).start()
                pltpu.make_async_copy(gqr.at[rng], gqr_hbm.at[rng], out_sem.at[1, b]).start()
            gacc[:, :lat] += dot_tn(probs_b, go_b) + dot_tn(grad_b, q_b)
            gacc[:, lat:] += dot_tn(grad_b, qr_b)
            return unused

        lax.fori_loop(0, count, step, 0)
        part[pl.ds(g * width, width), :] = gacc[...].astype(jnp.bfloat16)
        for dist in ORDER[g * GROUP : (g + 1) * GROUP]:
            for turn in range(n_head):
                if dist == 0 and turn == 0:
                    continue

                @pl.when(me >= dist)
                def _():
                    part_copy(dist, turn).start()

    total[...] = part[pl.ds(pl.multiple_of(my_head * piece, piece), piece), :].astype(jnp.float32)
    for dist in ORDER:
        for turn in range(n_head):
            if dist == 0 and turn == 0:
                continue

            @pl.when(me + dist < n_ctx)
            def _():
                part_copy(dist, turn).wait_recv()
                total[...] += recv[dist * n_head + turn].astype(jnp.float32)

    gkv_out[...] = total[...].astype(jnp.bfloat16)
    for dist in ORDER:

        if dist:

            @pl.when(me + dist < n_ctx)
            def _():
                kv_copy(dist).wait_send()

        for turn in range(n_head):
            if dist == 0 and turn == 0:
                continue

            @pl.when(me >= dist)
            def _():
                part_copy(dist, turn).wait_send()

    for b in range(count):
        rng = pl.ds(b * block, block)
        pltpu.make_async_copy(gq.at[rng], gq_hbm.at[rng], out_sem.at[0, b]).wait()
        pltpu.make_async_copy(gqr.at[rng], gqr_hbm.at[rng], out_sem.at[1, b]).wait()


def local(q_latent, q_rope, attn_out, grad_out, log_total, latent, key_rope, doc_start):
    n_ctx, n_head = lax.axis_size("ctx"), lax.axis_size("head")
    tok, heads, lat = q_latent.shape
    rows = tok * heads
    rope = key_rope.shape[1]
    wide = lat + 128
    block = min(BLOCK, rows)
    count = rows // block
    piece = tok // n_head
    width = GROUP * tok
    qr = jnp.pad(q_rope.reshape(rows, rope), ((0, 0), (0, 128 - rope)))
    kv = jnp.concatenate([latent, jnp.pad(key_rope, ((0, 0), (0, 128 - rope)))], axis=1)
    lt = jnp.broadcast_to((log_total * LOG2E).reshape(rows, 1), (rows, 128))
    starts = jnp.broadcast_to(doc_start[:, None], (tok, tok))
    bf, f32 = jnp.bfloat16, jnp.float32
    hbm = pl.BlockSpec(memory_space=pl.ANY)
    vmem = pl.BlockSpec(memory_space=pltpu.VMEM)
    gq, gqr, gkv = pl.pallas_call(
        functools.partial(kernel, n_ctx, n_head, tok, heads, lat),
        out_shape=(
            jax.ShapeDtypeStruct((rows, lat), bf),
            jax.ShapeDtypeStruct((rows, 128), bf),
            jax.ShapeDtypeStruct((piece, wide), bf),
        ),
        in_specs=[hbm] * 5 + [vmem] * 2,
        out_specs=(hbm, hbm, vmem),
        scratch_shapes=[
            pltpu.VMEM((rows, lat), bf),
            pltpu.VMEM((rows, 128), bf),
            pltpu.VMEM((rows, lat), bf),
            pltpu.VMEM((rows, lat), bf),
            pltpu.VMEM((rows, 128), f32),
            pltpu.VMEM((rows, 128), f32),
            pltpu.VMEM((SPAN * tok, wide), bf),
            pltpu.VMEM((SPAN // GROUP, tok, width), f32),
            pltpu.VMEM((rows, wide), f32),
            pltpu.VMEM((width, wide), f32),
            pltpu.VMEM((SPAN * tok, wide), bf),
            pltpu.VMEM((SPAN * n_head, piece, wide), bf),
            pltpu.VMEM((piece, wide), f32),
            pltpu.VMEM((rows, lat), bf),
            pltpu.VMEM((rows, 128), bf),
            pltpu.SemaphoreType.DMA((5, count)),
            pltpu.SemaphoreType.DMA((2, count)),
            pltpu.SemaphoreType.DMA((SPAN,)),
            pltpu.SemaphoreType.DMA((SPAN,)),
            pltpu.SemaphoreType.DMA((SPAN * n_head,)),
            pltpu.SemaphoreType.DMA((SPAN * n_head,)),
        ],
        compiler_params=pltpu.CompilerParams(
            collective_id=0, has_side_effects=True, vmem_limit_bytes=56 * 2**20
        ),
    )(
        q_latent.reshape(rows, lat),
        qr,
        attn_out.reshape(rows, lat),
        grad_out.reshape(rows, lat),
        lt,
        kv,
        starts,
    )
    return (
        gq.reshape(tok, heads, lat),
        gqr[:, :rope].reshape(tok, heads * rope),
        gkv[:, :lat],
        gkv[:, lat : lat + rope],
    )


def solution(mesh):
    in_specs = (
        P("ctx", "head", None),
        P("ctx", "head"),
        P("ctx", "head", None),
        P("ctx", "head", None),
        P("ctx", "head"),
        P("ctx", None),
        P("ctx", None),
        P("ctx"),
    )
    out_specs = (
        P("ctx", "head", None),
        P("ctx", "head"),
        P(("ctx", "head"), None),
        P(("ctx", "head"), None),
    )
    return jax.shard_map(local, mesh=mesh, in_specs=in_specs, out_specs=out_specs, check_vma=False)
```

```python
import functools

import jax
import jax.numpy as jnp
from jax import lax
from jax.experimental import pallas as pl
from jax.experimental.pallas import tpu as pltpu
from jax.sharding import PartitionSpec as P

ROPE = 64
NOPE = 128
LEVELS = 3
SPAN = 2**LEVELS
SCALE = (NOPE + ROPE) ** (-0.5)
LOG2E = 1.4426950408889634
ORDER = (1, 2, 3, 0)
BLOCK = 1024
PAIR = 2
HIDDEN = -1e30
MESH = pl.DeviceIdType.MESH


def dot_nt(a, b):
    return lax.dot_general(a, b, (((1,), (1,)), ((), ())), preferred_element_type=jnp.float32)


def dot_tn(a, b):
    return lax.dot_general(a, b, (((0,), (0,)), ((), ())), preferred_element_type=jnp.float32)


def dot_nn(a, b):
    return lax.dot_general(a, b, (((1,), (0,)), ((), ())), preferred_element_type=jnp.float32)


def kernel(
    n_ctx,
    n_head,
    tok,
    heads,
    lat,
    q_hbm,
    ao_hbm,
    go_hbm,
    q_rope,
    log_total,
    latent,
    key_rope,
    starts,
    gq_hbm,
    gqr_out,
    glat_out,
    grope_out,
    q,
    qr,
    go,
    ao,
    lt,
    delta,
    kv_own,
    kv,
    bias,
    acc,
    gacc,
    part,
    mate,
    send,
    recv,
    total,
    gq,
    gqr,
    in_sem,
    out_sem,
    kv_send,
    kv_recv,
    fw_send,
    fw_recv,
    m_send,
    m_recv,
    p_send,
    p_recv,
):
    me = lax.axis_index("ctx")
    my_head = lax.axis_index("head")
    rows = tok * heads
    block = min(BLOCK, rows)
    count = rows // block
    tok_blk = block // heads
    piece = tok // n_head
    width = PAIR * tok
    groups = SPAN // PAIR
    side = lax.rem(me, 2)
    partner = me + 1 - 2 * side
    chip = me // 2
    ahead = jnp.where(side == 0, 1, SPAN - 1)
    back = jnp.where(side == 0, SPAN - 1, 1)

    barrier = pltpu.get_barrier_semaphore()
    for dist in range(-(SPAN - 1), SPAN):
        for turn in range(n_head):
            if dist == 0 and turn == 0:
                continue

            @pl.when((me + dist >= 0) & (me + dist < n_ctx))
            def _():
                pl.semaphore_signal(
                    barrier,
                    inc=1,
                    device_id=(me + dist, lax.rem(my_head + turn, n_head)),
                    device_id_type=MESH,
                )

    def load(b):
        rng = pl.ds(b * block, block)
        return [
            pltpu.make_async_copy(src.at[rng], dst.at[rng], in_sem.at[i, b])
            for i, (src, dst) in enumerate(
                ((go_hbm, go), (ao_hbm, ao), (q_hbm, q))
            )
        ]

    for b in range(count):
        for copy in load(b):
            copy.start()

    rope_width = key_rope.shape[1]
    pair = 128 // rope_width
    key_wide = key_rope[...].astype(jnp.float32)
    kv_own[:, :lat] = latent[...]
    kv_own[:, lat:] = jnp.concatenate([key_wide] * pair, axis=1).astype(jnp.bfloat16)

    reach = jnp.minimum(me, SPAN - 1) + jnp.minimum(n_ctx - 1 - me, SPAN - 1) + 1
    pl.semaphore_wait(barrier, reach * n_head - 1)

    def tile_at(k, which):
        return pl.ds(pl.multiple_of((k * PAIR + which) * tok, tok), tok)

    def kv_copy(k):
        return pltpu.make_async_remote_copy(
            src_ref=kv_own,
            dst_ref=kv.at[tile_at(k, side)],
            send_sem=kv_send.at[k],
            recv_sem=kv_recv.at[k],
            device_id=(me + (PAIR * k if k else ahead), my_head),
            device_id_type=MESH,
        )

    def forward(k):
        return pltpu.make_async_remote_copy(
            src_ref=kv.at[tile_at(k, side)],
            dst_ref=kv.at[tile_at(k, side)],
            send_sem=fw_send.at[k],
            recv_sem=fw_recv.at[k],
            device_id=(partner, my_head),
            device_id_type=MESH,
        )

    def sends_kv(k):
        return me + (PAIR * k if k else ahead) < n_ctx

    def gets_kv(k):
        return me >= (PAIR * k if k else back)

    for k in ORDER:

        @pl.when(sends_kv(k))
        def _():
            kv_copy(k).start()

    kv[tile_at(0, side), :] = kv_own[...]

    @pl.when(me < back)
    def _():
        kv[tile_at(0, 1 - side), :] = jnp.zeros((tok, kv.shape[1]), kv.dtype)

    for k in range(1, groups):

        @pl.when(chip < k)
        def _():
            kv[pl.ds(k * width, width), :] = jnp.zeros((width, kv.shape[1]), kv.dtype)

    def pass_on(k):
        if k:

            @pl.when(gets_kv(k))
            def _():
                kv_copy(k).wait_recv()
                forward(k).start()

    part_of = lax.broadcasted_iota(jnp.int32, (tok, 128), 1) // rope_width
    for head in range(heads):
        lanes = pl.ds((head // pair) * 128, 128)
        own = jnp.where(part_of == head % pair, q_rope[:, lanes].astype(jnp.float32), 0.0)
        qr[pl.ds(head, tok, stride=heads), :] = own
    lt_wide = jnp.broadcast_to((log_total[...] * LOG2E)[:, :, None], (tok, heads, 128))
    lt[...] = lt_wide.reshape(rows, 128)
    first = jnp.broadcast_to(starts[...].astype(jnp.float32), (tok, tok)).T.astype(jnp.int32)
    query_pos = me * tok + lax.broadcasted_iota(jnp.int32, (tok, tok), 0)
    lane = lax.broadcasted_iota(jnp.int32, (tok, tok), 1)
    for k in range(groups):
        for which in range(PAIR):
            tile = PAIR * (chip - k) + which
            if k == 0 and which:
                tile = jnp.where(side == 0, me - (SPAN - 1), me)
            key_pos = tile * tok + lane
            seen = (key_pos >= first) & (key_pos <= query_pos)
            bias[k, :, pl.ds(which * tok, tok)] = jnp.where(seen, 0.0, HIDDEN)

    def mate_copy(k):
        return pltpu.make_async_remote_copy(
            src_ref=part.at[tile_at(k, 1 - side)],
            dst_ref=mate.at[k],
            send_sem=m_send.at[k],
            recv_sem=m_recv.at[k],
            device_id=(partner, my_head),
            device_id_type=MESH,
        )

    def part_copy(k, turn):
        target = lax.rem(my_head + turn, n_head)
        if k in (0, groups):
            which = side if k == 0 else 1 - side
            src = part.at[pl.ds(pl.multiple_of(which * tok + target * piece, piece), piece)]
        else:
            src = send.at[k, pl.ds(pl.multiple_of(target * piece, piece), piece)]
        return pltpu.make_async_remote_copy(
            src_ref=src,
            dst_ref=recv.at[k * n_head + turn],
            send_sem=p_send.at[k * n_head + turn],
            recv_sem=p_recv.at[k * n_head + turn],
            device_id=(me - (back if k == groups else PAIR * k), target),
            device_id_type=MESH,
        )

    def sends_part(k):
        return me >= (back if k == groups else PAIR * k)

    def gets_part(k):
        return me + (ahead if k == groups else PAIR * k) < n_ctx

    def start_parts(k):
        for turn in range(n_head):
            if k or turn:

                @pl.when(sends_part(k))
                def _():
                    part_copy(k, turn).start()

    def join(k):
        @pl.when(sends_part(k))
        def _():
            mate_copy(k).wait_recv()
            own = part[tile_at(k, side), :].astype(jnp.float32)
            send[k] = (own + mate[k].astype(jnp.float32)).astype(jnp.bfloat16)

        start_parts(k)

    def row_delta(b, unused):
        rng = pl.ds(pl.multiple_of(b * block, block), block)
        for copy in load(b):
            copy.wait()
        d = jnp.sum(
            go[rng, :].astype(jnp.float32) * ao[rng, :].astype(jnp.float32), axis=1, keepdims=True
        )
        delta[rng, :] = jnp.broadcast_to(d * SCALE, (block, 128))
        return unused

    lax.fori_loop(0, count, row_delta, 0)
    pass_on(ORDER[0])
    mid = min(1, count - 1)
    for turn_at, k in enumerate(ORDER):
        earlier = ORDER[turn_at - 1] if turn_at else None
        later = ORDER[turn_at + 1] if turn_at < groups - 1 else None

        @pl.when(gets_kv(k))
        def _():
            if k:
                forward(k).wait_recv()
            else:
                kv_copy(k).wait_recv()

        gacc[...] = jnp.zeros_like(gacc)

        def step(b, unused):
            start = pl.multiple_of(b * block, block)
            rng = pl.ds(start, block)

            @pl.when(b == mid)
            def _():
                if later is not None:
                    pass_on(later)
                if earlier:
                    join(earlier)

            keys = kv[pl.ds(k * width, width), :]
            q_b, qr_b, go_b = q[rng, :], qr[rng, :].astype(jnp.bfloat16), go[rng, :]
            scores = dot_nt(q_b, keys[:, :lat]) + dot_nt(qr_b, keys[:, lat:])
            grad_probs = dot_nt(go_b, keys[:, :lat])
            hide = bias[k, pl.ds(pl.multiple_of(b * tok_blk, tok_blk), tok_blk), :]
            hide = jnp.broadcast_to(hide[:, None, :], (tok_blk, heads, width)).reshape(block, width)
            times = width // 128
            lt_b = jnp.concatenate([lt[rng, :]] * times, axis=1)
            d_b = jnp.concatenate([delta[rng, :]] * times, axis=1)
            probs = jnp.exp2(scores * (SCALE * LOG2E) - lt_b + hide)
            grads = probs * (grad_probs * SCALE - d_b)
            probs_b = probs.astype(jnp.bfloat16)
            grad_b = grads.astype(jnp.bfloat16)
            gq_b = dot_nn(grad_b, keys)
            if earlier is not None:
                gq_b = acc[rng, :] + gq_b
            if later is not None:
                acc[rng, :] = gq_b
            else:
                gq[rng, :] = gq_b[:, :lat].astype(jnp.bfloat16)
                gqr[rng, :] = gq_b[:, lat:]
                pltpu.make_async_copy(gq.at[rng], gq_hbm.at[rng], out_sem.at[b]).start()
            gacc[:, :lat] += dot_tn(probs_b, go_b) + dot_tn(grad_b, q_b)
            gacc[:, lat:] += dot_tn(grad_b, qr_b)
            return unused

        lax.fori_loop(0, count, step, 0)
        part[pl.ds(k * width, width), :] = gacc[...].astype(jnp.bfloat16)
        if k:

            @pl.when(sends_part(k))
            def _():
                mate_copy(k).start()

        else:
            start_parts(groups)
            start_parts(0)
    if ORDER[-1]:
        join(ORDER[-1])

    for tile in range(heads // pair):
        own = gqr[pl.ds(tile * pair, tok, stride=heads), :]
        for i in range(1, pair):
            own = jnp.where(part_of == i, gqr[pl.ds(tile * pair + i, tok, stride=heads), :], own)
        gqr_out[:, pl.ds(tile * 128, 128)] = own.astype(jnp.bfloat16)

    mine = pl.ds(pl.multiple_of(side * tok + my_head * piece, piece), piece)
    total[...] = part[mine, :].astype(jnp.float32)
    for k in ORDER[:-1] + (ORDER[-1], groups):
        for turn in range(n_head):
            if k or turn:

                @pl.when(gets_part(k))
                def _():
                    part_copy(k, turn).wait_recv()
                    total[...] += recv[k * n_head + turn].astype(jnp.float32)

    glat_out[...] = total[:, :lat].astype(jnp.bfloat16)
    rope_sum = total[:, lat : lat + rope_width]
    for i in range(1, pair):
        rope_sum += total[:, lat + i * rope_width : lat + (i + 1) * rope_width]
    grope_out[...] = rope_sum.astype(jnp.bfloat16)
    for k in range(groups):

        @pl.when(sends_kv(k))
        def _():
            kv_copy(k).wait_send()

        if k:

            @pl.when(gets_kv(k))
            def _():
                forward(k).wait_send()
                mate_copy(k).wait_send()

    for k in range(groups + 1):
        for turn in range(n_head):
            if k or turn:

                @pl.when(sends_part(k))
                def _():
                    part_copy(k, turn).wait_send()

    for b in range(count):
        rng = pl.ds(b * block, block)
        pltpu.make_async_copy(gq.at[rng], gq_hbm.at[rng], out_sem.at[b]).wait()


def local(q_latent, q_rope, attn_out, grad_out, log_total, latent, key_rope, doc_start):
    n_ctx, n_head = lax.axis_size("ctx"), lax.axis_size("head")
    tok, heads, lat = q_latent.shape
    rows = tok * heads
    rope = key_rope.shape[1]
    wide = lat + 128
    block = min(BLOCK, rows)
    count = rows // block
    piece = tok // n_head
    width = PAIR * tok
    slots = (SPAN // PAIR + 1) * n_head
    bf, f32 = jnp.bfloat16, jnp.float32
    hbm = pl.BlockSpec(memory_space=pl.ANY)
    vmem = pl.BlockSpec(memory_space=pltpu.VMEM)
    gq, gqr, glat, grope = pl.pallas_call(
        functools.partial(kernel, n_ctx, n_head, tok, heads, lat),
        out_shape=(
            jax.ShapeDtypeStruct((rows, lat), bf),
            jax.ShapeDtypeStruct(q_rope.shape, bf),
            jax.ShapeDtypeStruct((piece, lat), bf),
            jax.ShapeDtypeStruct((piece, rope), bf),
        ),
        in_specs=[hbm] * 3 + [vmem] * 5,
        out_specs=(hbm, vmem, vmem, vmem),
        scratch_shapes=[
            pltpu.VMEM((rows, lat), bf),
            pltpu.VMEM((rows, 128), f32),
            pltpu.VMEM((rows, lat), bf),
            pltpu.VMEM((rows, lat), bf),
            pltpu.VMEM((rows, 128), f32),
            pltpu.VMEM((rows, 128), f32),
            pltpu.VMEM((tok, wide), bf),
            pltpu.VMEM((SPAN * tok, wide), bf),
            pltpu.VMEM((SPAN // PAIR, tok, width), f32),
            pltpu.VMEM((rows, wide), f32),
            pltpu.VMEM((width, wide), f32),
            pltpu.VMEM((SPAN * tok, wide), bf),
            pltpu.VMEM((SPAN // PAIR, tok, wide), bf),
            pltpu.VMEM((SPAN // PAIR, tok, wide), bf),
            pltpu.VMEM((slots, piece, wide), bf),
            pltpu.VMEM((piece, wide), f32),
            pltpu.VMEM((rows, lat), bf),
            pltpu.VMEM((rows, 128), f32),
            pltpu.SemaphoreType.DMA((3, count)),
            pltpu.SemaphoreType.DMA((count,)),
            pltpu.SemaphoreType.DMA((SPAN // PAIR,)),
            pltpu.SemaphoreType.DMA((SPAN // PAIR,)),
            pltpu.SemaphoreType.DMA((SPAN // PAIR,)),
            pltpu.SemaphoreType.DMA((SPAN // PAIR,)),
            pltpu.SemaphoreType.DMA((SPAN // PAIR,)),
            pltpu.SemaphoreType.DMA((SPAN // PAIR,)),
            pltpu.SemaphoreType.DMA((slots,)),
            pltpu.SemaphoreType.DMA((slots,)),
        ],
        compiler_params=pltpu.CompilerParams(
            collective_id=0, has_side_effects=True, vmem_limit_bytes=56 * 2**20
        ),
    )(
        q_latent.reshape(rows, lat),
        attn_out.reshape(rows, lat),
        grad_out.reshape(rows, lat),
        q_rope,
        log_total,
        latent,
        key_rope,
        doc_start.reshape(1, tok),
    )
    return gq.reshape(tok, heads, lat), gqr, glat, grope


def solution(mesh):
    in_specs = (
        P("ctx", "head", None),
        P("ctx", "head"),
        P("ctx", "head", None),
        P("ctx", "head", None),
        P("ctx", "head"),
        P("ctx", None),
        P("ctx", None),
        P("ctx"),
    )
    out_specs = (
        P("ctx", "head", None),
        P("ctx", "head"),
        P(("ctx", "head"), None),
        P(("ctx", "head"), None),
    )
    return jax.shard_map(local, mesh=mesh, in_specs=in_specs, out_specs=out_specs, check_vma=False)
```

```python
import functools

import jax
import jax.numpy as jnp
from jax import lax
from jax.experimental import pallas as pl
from jax.experimental.pallas import tpu as pltpu
from jax.sharding import PartitionSpec as P

ROPE = 64
NOPE = 128
LEVELS = 3
SPAN = 2**LEVELS
SCALE = (NOPE + ROPE) ** (-0.5)
LOG2E = 1.4426950408889634
ORDER = (1, 2, 3, 0)
BLOCK = 2048
PAIR = 2
HIDDEN = -1e30
MESH = pl.DeviceIdType.MESH


def dot_nt(a, b):
    return lax.dot_general(a, b, (((1,), (1,)), ((), ())), preferred_element_type=jnp.float32)


def dot_tn(a, b):
    return lax.dot_general(a, b, (((0,), (0,)), ((), ())), preferred_element_type=jnp.float32)


def dot_nn(a, b):
    return lax.dot_general(a, b, (((1,), (0,)), ((), ())), preferred_element_type=jnp.float32)


def kernel(
    n_ctx,
    n_head,
    tok,
    heads,
    lat,
    q_hbm,
    ao_hbm,
    go_hbm,
    q_rope,
    log_total,
    latent,
    key_rope,
    starts,
    gq_hbm,
    gqr_out,
    glat_out,
    grope_out,
    q,
    qr,
    go,
    ao,
    lt,
    delta,
    kv_own,
    kv,
    bias,
    acc,
    gacc,
    part,
    mate,
    send,
    recv,
    total,
    gq,
    gqr,
    in_sem,
    out_sem,
    kv_send,
    kv_recv,
    fw_send,
    fw_recv,
    m_send,
    m_recv,
    p_send,
    p_recv,
):
    me = lax.axis_index("ctx")
    my_head = lax.axis_index("head")
    rows = tok * heads
    block = min(BLOCK, rows)
    count = rows // block
    tok_blk = block // heads
    piece = tok // n_head
    width = PAIR * tok
    groups = SPAN // PAIR
    side = lax.rem(me, 2)
    partner = me + 1 - 2 * side
    chip = me // 2
    ahead = jnp.where(side == 0, 1, SPAN - 1)
    back = jnp.where(side == 0, SPAN - 1, 1)

    barrier = pltpu.get_barrier_semaphore()
    for dist in range(-(SPAN - 1), SPAN):
        for turn in range(n_head):
            if dist == 0 and turn == 0:
                continue

            @pl.when((me + dist >= 0) & (me + dist < n_ctx))
            def _():
                pl.semaphore_signal(
                    barrier,
                    inc=1,
                    device_id=(me + dist, lax.rem(my_head + turn, n_head)),
                    device_id_type=MESH,
                )

    def load(b):
        rng = pl.ds(b * block, block)
        return [
            pltpu.make_async_copy(src.at[rng], dst.at[rng], in_sem.at[i, b])
            for i, (src, dst) in enumerate(
                ((go_hbm, go), (ao_hbm, ao), (q_hbm, q))
            )
        ]

    for b in range(count):
        for copy in load(b):
            copy.start()

    rope_width = key_rope.shape[0]
    pair = 128 // rope_width
    key_wide = key_rope[...].astype(jnp.float32).T
    kv_own[:, :lat] = latent[...]
    kv_own[:, lat:] = jnp.concatenate([key_wide] * pair, axis=1).astype(jnp.bfloat16)

    reach = jnp.minimum(me, SPAN - 1) + jnp.minimum(n_ctx - 1 - me, SPAN - 1) + 1
    pl.semaphore_wait(barrier, reach * n_head - 1)

    def tile_at(k, which):
        return pl.ds(pl.multiple_of((k * PAIR + which) * tok, tok), tok)

    def kv_copy(k):
        return pltpu.make_async_remote_copy(
            src_ref=kv_own,
            dst_ref=kv.at[tile_at(k, side)],
            send_sem=kv_send.at[k],
            recv_sem=kv_recv.at[k],
            device_id=(me + (PAIR * k if k else ahead), my_head),
            device_id_type=MESH,
        )

    def forward(k):
        return pltpu.make_async_remote_copy(
            src_ref=kv.at[tile_at(k, side)],
            dst_ref=kv.at[tile_at(k, side)],
            send_sem=fw_send.at[k],
            recv_sem=fw_recv.at[k],
            device_id=(partner, my_head),
            device_id_type=MESH,
        )

    def sends_kv(k):
        return me + (PAIR * k if k else ahead) < n_ctx

    def gets_kv(k):
        return me >= (PAIR * k if k else back)

    for k in ORDER:

        @pl.when(sends_kv(k))
        def _():
            kv_copy(k).start()

    kv[tile_at(0, side), :] = kv_own[...]

    @pl.when(me < back)
    def _():
        kv[tile_at(0, 1 - side), :] = jnp.zeros((tok, kv.shape[1]), kv.dtype)

    for k in range(1, groups):

        @pl.when(chip < k)
        def _():
            kv[pl.ds(k * width, width), :] = jnp.zeros((width, kv.shape[1]), kv.dtype)

    def pass_on(k):
        if k:

            @pl.when(gets_kv(k))
            def _():
                kv_copy(k).wait_recv()
                forward(k).start()

    part_of = lax.broadcasted_iota(jnp.int32, (tok, 128), 1) // rope_width
    for head in range(heads):
        lanes = pl.ds((head // pair) * 128, 128)
        own = jnp.where(part_of == head % pair, q_rope[:, lanes].astype(jnp.float32), 0.0)
        qr[pl.ds(head, tok, stride=heads), :] = own
    lt_wide = jnp.broadcast_to((log_total[...] * LOG2E).T[:, :, None], (tok, heads, 128))
    lt[...] = lt_wide.reshape(rows, 128)
    first = jnp.broadcast_to(starts[...].astype(jnp.float32), (tok, tok)).T.astype(jnp.int32)
    query_pos = me * tok + lax.broadcasted_iota(jnp.int32, (tok, tok), 0)
    lane = lax.broadcasted_iota(jnp.int32, (tok, tok), 1)
    for k in range(groups):
        for which in range(PAIR):
            tile = PAIR * (chip - k) + which
            if k == 0 and which:
                tile = jnp.where(side == 0, me - (SPAN - 1), me)
            key_pos = tile * tok + lane
            seen = (key_pos >= first) & (key_pos <= query_pos)
            bias[k, :, pl.ds(which * tok, tok)] = jnp.where(seen, 0.0, HIDDEN)

    def mate_copy(k):
        return pltpu.make_async_remote_copy(
            src_ref=part.at[tile_at(k, 1 - side)],
            dst_ref=mate.at[k],
            send_sem=m_send.at[k],
            recv_sem=m_recv.at[k],
            device_id=(partner, my_head),
            device_id_type=MESH,
        )

    def part_copy(k, turn):
        target = lax.rem(my_head + turn, n_head)
        if k in (0, groups):
            which = side if k == 0 else 1 - side
            src = part.at[pl.ds(pl.multiple_of(which * tok + target * piece, piece), piece)]
        else:
            src = send.at[k, pl.ds(pl.multiple_of(target * piece, piece), piece)]
        return pltpu.make_async_remote_copy(
            src_ref=src,
            dst_ref=recv.at[k * n_head + turn],
            send_sem=p_send.at[k * n_head + turn],
            recv_sem=p_recv.at[k * n_head + turn],
            device_id=(me - (back if k == groups else PAIR * k), target),
            device_id_type=MESH,
        )

    def sends_part(k):
        return me >= (back if k == groups else PAIR * k)

    def gets_part(k):
        return me + (ahead if k == groups else PAIR * k) < n_ctx

    def start_parts(k):
        for turn in range(n_head):
            if k or turn:

                @pl.when(sends_part(k))
                def _():
                    part_copy(k, turn).start()

    def join(k):
        @pl.when(sends_part(k))
        def _():
            mate_copy(k).wait_recv()
            own = part[tile_at(k, side), :].astype(jnp.float32)
            send[k] = (own + mate[k].astype(jnp.float32)).astype(jnp.bfloat16)

        start_parts(k)

    def row_delta(b, unused):
        rng = pl.ds(pl.multiple_of(b * block, block), block)
        for copy in load(b):
            copy.wait()
        d = jnp.sum(
            go[rng, :].astype(jnp.float32) * ao[rng, :].astype(jnp.float32), axis=1, keepdims=True
        )
        delta[rng, :] = jnp.broadcast_to(d * SCALE, (block, 128))
        return unused

    lax.fori_loop(0, count, row_delta, 0)
    pass_on(ORDER[0])
    mid = min(1, count - 1)
    for turn_at, k in enumerate(ORDER):
        earlier = ORDER[turn_at - 1] if turn_at else None
        later = ORDER[turn_at + 1] if turn_at < groups - 1 else None

        @pl.when(gets_kv(k))
        def _():
            if k:
                forward(k).wait_recv()
            else:
                kv_copy(k).wait_recv()

        gacc[...] = jnp.zeros_like(gacc)

        def step(b, unused):
            start = pl.multiple_of(b * block, block)
            rng = pl.ds(start, block)

            @pl.when(b == mid)
            def _():
                if later is not None:
                    pass_on(later)
                if earlier:
                    join(earlier)

            keys = kv[pl.ds(k * width, width), :]
            q_b, qr_b, go_b = q[rng, :], qr[rng, :].astype(jnp.bfloat16), go[rng, :]
            scores = dot_nt(q_b, keys[:, :lat]) + dot_nt(qr_b, keys[:, lat:])
            grad_probs = dot_nt(go_b, keys[:, :lat])
            hide = bias[k, pl.ds(pl.multiple_of(b * tok_blk, tok_blk), tok_blk), :]
            hide = jnp.broadcast_to(hide[:, None, :], (tok_blk, heads, width)).reshape(block, width)
            times = width // 128
            lt_b = jnp.concatenate([lt[rng, :]] * times, axis=1)
            d_b = jnp.concatenate([delta[rng, :]] * times, axis=1)
            probs = jnp.exp2(scores * (SCALE * LOG2E) - lt_b + hide)
            grads = probs * (grad_probs * SCALE - d_b)
            probs_b = probs.astype(jnp.bfloat16)
            grad_b = grads.astype(jnp.bfloat16)
            gq_b = dot_nn(grad_b, keys)
            if earlier is not None:
                gq_b = acc[rng, :] + gq_b
            if later is not None:
                acc[rng, :] = gq_b
            else:
                gq[rng, :] = gq_b[:, :lat].astype(jnp.bfloat16)
                gqr[rng, :] = gq_b[:, lat:]
                pltpu.make_async_copy(gq.at[rng], gq_hbm.at[rng], out_sem.at[b]).start()
            gacc[:, :lat] += dot_tn(probs_b, go_b) + dot_tn(grad_b, q_b)
            gacc[:, lat:] += dot_tn(grad_b, qr_b)
            return unused

        lax.fori_loop(0, count, step, 0)
        part[pl.ds(k * width, width), :] = gacc[...].astype(jnp.bfloat16)
        if k:

            @pl.when(sends_part(k))
            def _():
                mate_copy(k).start()

        else:
            start_parts(groups)
            start_parts(0)
    if ORDER[-1]:
        join(ORDER[-1])

    for tile in range(heads // pair):
        own = gqr[pl.ds(tile * pair, tok, stride=heads), :]
        for i in range(1, pair):
            own = jnp.where(part_of == i, gqr[pl.ds(tile * pair + i, tok, stride=heads), :], own)
        gqr_out[:, pl.ds(tile * 128, 128)] = own.astype(jnp.bfloat16)

    mine = pl.ds(pl.multiple_of(side * tok + my_head * piece, piece), piece)
    total[...] = part[mine, :].astype(jnp.float32)
    for k in ORDER[:-1] + (ORDER[-1], groups):
        for turn in range(n_head):
            if k or turn:

                @pl.when(gets_part(k))
                def _():
                    part_copy(k, turn).wait_recv()
                    total[...] += recv[k * n_head + turn].astype(jnp.float32)

    glat_out[...] = total[:, :lat].astype(jnp.bfloat16)
    rope_sum = total[:, lat : lat + rope_width]
    for i in range(1, pair):
        rope_sum += total[:, lat + i * rope_width : lat + (i + 1) * rope_width]
    grope_out[...] = rope_sum.astype(jnp.bfloat16)
    for k in range(groups):

        @pl.when(sends_kv(k))
        def _():
            kv_copy(k).wait_send()

        if k:

            @pl.when(gets_kv(k))
            def _():
                forward(k).wait_send()
                mate_copy(k).wait_send()

    for k in range(groups + 1):
        for turn in range(n_head):
            if k or turn:

                @pl.when(sends_part(k))
                def _():
                    part_copy(k, turn).wait_send()

    for b in range(count):
        rng = pl.ds(b * block, block)
        pltpu.make_async_copy(gq.at[rng], gq_hbm.at[rng], out_sem.at[b]).wait()


def local(q_latent, q_rope, attn_out, grad_out, log_total, latent, key_rope, doc_start):
    n_ctx, n_head = lax.axis_size("ctx"), lax.axis_size("head")
    tok, heads, lat = q_latent.shape
    rows = tok * heads
    rope = key_rope.shape[1]
    wide = lat + 128
    block = min(BLOCK, rows)
    count = rows // block
    piece = tok // n_head
    width = PAIR * tok
    slots = (SPAN // PAIR + 1) * n_head
    bf, f32 = jnp.bfloat16, jnp.float32
    hbm = pl.BlockSpec(memory_space=pl.ANY)
    vmem = pl.BlockSpec(memory_space=pltpu.VMEM)
    gq, gqr, glat, grope = pl.pallas_call(
        functools.partial(kernel, n_ctx, n_head, tok, heads, lat),
        out_shape=(
            jax.ShapeDtypeStruct((rows, lat), bf),
            jax.ShapeDtypeStruct(q_rope.shape, bf),
            jax.ShapeDtypeStruct((piece, lat), bf),
            jax.ShapeDtypeStruct((piece, rope), bf),
        ),
        in_specs=[hbm] * 3 + [vmem] * 5,
        out_specs=(hbm, vmem, vmem, vmem),
        scratch_shapes=[
            pltpu.VMEM((rows, lat), bf),
            pltpu.VMEM((rows, 128), f32),
            pltpu.VMEM((rows, lat), bf),
            pltpu.VMEM((rows, lat), bf),
            pltpu.VMEM((rows, 128), f32),
            pltpu.VMEM((rows, 128), f32),
            pltpu.VMEM((tok, wide), bf),
            pltpu.VMEM((SPAN * tok, wide), bf),
            pltpu.VMEM((SPAN // PAIR, tok, width), f32),
            pltpu.VMEM((rows, wide), f32),
            pltpu.VMEM((width, wide), f32),
            pltpu.VMEM((SPAN * tok, wide), bf),
            pltpu.VMEM((SPAN // PAIR, tok, wide), bf),
            pltpu.VMEM((SPAN // PAIR, tok, wide), bf),
            pltpu.VMEM((slots, piece, wide), bf),
            pltpu.VMEM((piece, wide), f32),
            pltpu.VMEM((rows, lat), bf),
            pltpu.VMEM((rows, 128), f32),
            pltpu.SemaphoreType.DMA((3, count)),
            pltpu.SemaphoreType.DMA((count,)),
            pltpu.SemaphoreType.DMA((SPAN // PAIR,)),
            pltpu.SemaphoreType.DMA((SPAN // PAIR,)),
            pltpu.SemaphoreType.DMA((SPAN // PAIR,)),
            pltpu.SemaphoreType.DMA((SPAN // PAIR,)),
            pltpu.SemaphoreType.DMA((SPAN // PAIR,)),
            pltpu.SemaphoreType.DMA((SPAN // PAIR,)),
            pltpu.SemaphoreType.DMA((slots,)),
            pltpu.SemaphoreType.DMA((slots,)),
        ],
        compiler_params=pltpu.CompilerParams(
            collective_id=0, has_side_effects=True, vmem_limit_bytes=56 * 2**20
        ),
    )(
        q_latent.reshape(rows, lat),
        attn_out.reshape(rows, lat),
        grad_out.reshape(rows, lat),
        q_rope,
        log_total.T,
        latent,
        key_rope.T,
        doc_start.reshape(1, tok),
    )
    return gq.reshape(tok, heads, lat), gqr, glat, grope


def solution(mesh):
    in_specs = (
        P("ctx", "head", None),
        P("ctx", "head"),
        P("ctx", "head", None),
        P("ctx", "head", None),
        P("ctx", "head"),
        P("ctx", None),
        P("ctx", None),
        P("ctx"),
    )
    out_specs = (
        P("ctx", "head", None),
        P("ctx", "head"),
        P(("ctx", "head"), None),
        P(("ctx", "head"), None),
    )
    return jax.shard_map(local, mesh=mesh, in_specs=in_specs, out_specs=out_specs, check_vma=False)
```
